32 devices in a mesh: table: 16 (over z, y, x), segment: 2 (over core).
Axes of the slice: x: 2, y: 2, z: 4, core: 2. Of those that a mesh axis runs over, the one named last changes fastest.
Arguments:
- hidden: bfloat16 [2, 4096, 1280], P('segment', 'table'), may hold values from -6 to 6
- owner: int32 [2, 4096, 8], P('segment', 'table'), may hold values from 0 to 15, all different within a row; in each aligned block of 256 rows (0 to 255, 256 to 511, ..., all dimensions but the last counted through in order) at most 256 rows name the same one
- slot: int32 [2, 4096, 8], P('segment', 'table'), may hold values from 0 to 511
- memory_table: bfloat16 [2, 8192, 640], P('segment', 'table'), may hold values from -6 to 6
- key_weight: bfloat16 [2, 640, 1280], P('segment'), may hold values from -0.25 to 0.25
- value_weight: bfloat16 [2, 640, 1280], P('segment'), may hold values from -0.25 to 0.25
- conv_weight: float32 [2, 4, 1280], P('segment'), may hold values from -3 to 3
Outputs:
- passed: bfloat16 [2, 4096, 1280], P('segment', 'table')
The draws below stay inside these ranges and needn't reach their ends.
Inputs may be any that keep to these rules, and one draw needn't show every extreme that they name: `owner`: A token's 8 heads name different shards; among the tokens of one device no shard is named by more than 256 lookups, a bound that some block reaches.
All inputs are finite; a program needn't handle non-finite values.
Results may differ from the reference program's by a relative error of at most 0.0047.
Values may be sent and summed in bfloat16 or wider, within the bound.
A program may use at most 64 MiB of HBM per device.

```python
import math
import jax
import jax.numpy as jnp
import numpy as np
from jax import lax

D = 1280
DE = 640
HEADS = 8
KW = 4
CONV_DILATION = 3
TOK_DEV = 256
ROWS = 8192
SEQUENCE_TOKENS = 4096
ROWS_DEV = 512
MOST = 256
N_TABLE = 16
N_SEGMENT = 2


def with_ends(values, own_key, low, high):
    dims = values.shape
    place = [jax.random.randint(jax.random.fold_in(own_key, axis), (), 0, dims[axis]) for axis in range(len(dims))]
    values = values.at[tuple(place)].set(low)
    longest = dims.index(max(dims))
    place[longest] = (place[longest] + 1) % dims[longest]
    return values.at[tuple(place)].set(high)


def block_scale(own_key, shape, cuts, low, largest):
    def one(axis_at, shards_of):
        steps = jax.random.uniform(jax.random.fold_in(jax.random.fold_in(own_key, 6), axis_at), (shards_of,), jnp.float32, low / len(cuts), largest / len(cuts))
        return jnp.repeat(jnp.exp(steps), shape[axis_at] // shards_of).reshape((-1,) + (1,) * (len(shape) - axis_at - 1))

    level = one(*cuts[0])
    for cut in cuts[1:]:
        level = level * one(*cut)
    return level


def routed_block(own_key, own, number, rows, number_of, top, reach, skew):
    ranking = jax.random.permutation(own_key, number_of)
    heavy_load, ordinary = load_shares(number_of, rows * top, reach, skew, True), load_shares(number_of, rows * top, reach, skew, False)
    places = jnp.arange(number_of)

    def named(sizes, turn):
        used = int((sizes > 0).sum())
        fixed = max(1, used // 4)
        moved = fixed + (places - fixed + turn * (used - fixed)) % max(1, number_of - fixed)
        return jnp.zeros((number_of,), jnp.int32).at[ranking[jnp.where(places < fixed, places, moved)]].set(jnp.asarray(sizes, jnp.int32))

    sizes = jnp.where(number % 4 == 0, named(heavy_load, number // 4), named(ordinary, number - number // 4 - 1))
    mixed = jax.random.permutation(jax.random.fold_in(own, 3), number_of)
    giver, sink = mixed[0:number_of // 2 * 2:2], mixed[1:number_of // 2 * 2:2]
    room = jnp.minimum(sizes[giver] - 1, reach - sizes[sink]) // 2
    room = jnp.where((giver == ranking[0]) | (sink == ranking[0]) | (sizes[sink] == 0), 0, jnp.maximum(room, 0))
    moved = jax.random.randint(jax.random.fold_in(own, 4), (number_of // 2,), 0, 1 << 20) % (room + 1)
    sizes = sizes.at[giver].add(-moved).at[sink].add(moved)
    labels = jnp.searchsorted(jnp.cumsum(sizes), jnp.arange(rows * top), side="right").astype(jnp.int32)
    grid = labels.reshape(top, rows).T
    grid = grid[jax.random.permutation(jax.random.fold_in(own, 1), rows)]
    turn = jax.random.randint(jax.random.fold_in(own, 2), (rows, 1), 0, top)
    return jnp.take_along_axis(grid, (jnp.arange(top)[None, :] + turn) % top, axis=1)


def load_shares(count, total, bound, slope, full):
    weights = [(1 << 20) // math.isqrt(rank ** slope) + 1 for rank in range(1, count + 1)]
    largest = bound if full else min(bound, max(-(-total // count), total * weights[0] // sum(weights)))
    least = 1 if total - largest >= count - 1 else 0
    given, surplus = [largest] + [least] * (count - 1), total - largest - least * (count - 1)
    while surplus > 0:
        candidates = [i for i in range(1, count) if given[i] < largest] or [i for i in range(1, count) if given[i] < bound]
        pool, remaining = sum([weights[i] for i in candidates]), surplus
        for i in candidates:
            more = min(bound - given[i], max(1, remaining * weights[i] // pool), surplus)
            given[i] = given[i] + more
            surplus = surplus - more
    return np.array(given)


def centred(key, shape, width, most, cuts=(), dtype=jnp.bfloat16):
    values = jax.random.normal(key, shape, jnp.float32) * width
    if len(cuts) > 0:
        values = block_scale(key, shape, cuts, -0.22, 0.18) * values
    return jnp.clip(values, min=-most, max=most).astype(dtype)


def setup_inputs(seed: int = 0) -> dict:
    key_of = jax.random.split(jax.random.key(seed), 8)
    hidden = centred(key_of[0], (N_SEGMENT, SEQUENCE_TOKENS, D), 1.0, 6.0, ((0, 2), (1, 16)))
    owner_keys = jax.random.split(jax.random.fold_in(key_of[1], 1), N_SEGMENT * SEQUENCE_TOKENS // TOK_DEV)
    owner_turns = jax.random.permutation(jax.random.fold_in(key_of[1], 3), N_SEGMENT * SEQUENCE_TOKENS // TOK_DEV)
    owner = jax.vmap(lambda own, number: routed_block(jax.random.fold_in(key_of[1], 2), own, number, TOK_DEV, N_TABLE, HEADS, MOST, 2))(owner_keys, owner_turns).reshape((N_SEGMENT, SEQUENCE_TOKENS, HEADS))
    slot = with_ends(jax.random.randint(key_of[2], (N_SEGMENT, SEQUENCE_TOKENS, HEADS), 0, ROWS_DEV), jax.random.fold_in(key_of[2], 1), 0, ROWS_DEV - 1).astype(jnp.int32)
    memory_table = centred(key_of[3], (N_SEGMENT, ROWS, DE), 1.0, 6.0, ((0, 2), (1, 16)))
    key_weight = centred(key_of[4], (N_SEGMENT, DE, D), DE ** -0.5, 0.25, ((0, 2),))
    value_weight = centred(key_of[5], (N_SEGMENT, DE, D), DE ** -0.5, 0.25, ((0, 2),))
    conv_weight = centred(key_of[6], (N_SEGMENT, KW, D), 0.5, 3.0, ((0, 2),), jnp.float32)
    return dict(hidden=hidden, owner=owner, slot=slot, memory_table=memory_table, key_weight=key_weight, value_weight=value_weight, conv_weight=conv_weight)


def rms_scale(values):
    return values * lax.rsqrt(lax.optimization_barrier(jnp.mean(values * values, axis=-1, keepdims=True)) + 1e-06)

def one_section(operands):
    states, owners, slot_rows, table_rows, key_proj, value_proj, taps = operands
    global_ids = (owners * ROWS_DEV + slot_rows).astype(jnp.int32)
    memory = jnp.zeros((SEQUENCE_TOKENS, DE), jnp.float32)
    for head_index in range(HEADS):
        memory = memory + table_rows[global_ids[:, head_index]].astype(jnp.float32)
    packed = memory.astype(jnp.bfloat16)
    keys_out = jnp.dot(packed, key_proj, preferred_element_type=jnp.float32)
    values_out = jnp.dot(packed, value_proj, preferred_element_type=jnp.float32)
    states_float = states.astype(jnp.float32)
    affinity = lax.optimization_barrier(jnp.sum(rms_scale(states_float) * rms_scale(keys_out), axis=-1, keepdims=True)) / math.sqrt(D)
    gated_value = jax.nn.sigmoid(affinity) * values_out
    scaled_states = rms_scale(gated_value)
    convolved = jnp.zeros((SEQUENCE_TOKENS, D), jnp.float32)
    for kernel_tap_index in range(KW):
        lagged_states = jnp.pad(scaled_states, ((kernel_tap_index * CONV_DILATION, 0), (0, 0)))[:SEQUENCE_TOKENS]
        convolved = convolved + taps[kernel_tap_index] * lagged_states
    branch_out = jax.nn.silu(convolved) + gated_value
    return (states_float + branch_out).astype(jnp.bfloat16)

def reference(hidden, owner, slot, memory_table, key_weight, value_weight, conv_weight):
    result = lax.map(one_section, (hidden, owner, slot, memory_table, key_weight, value_weight, conv_weight))
    return jnp.roll(result, 1, axis=0)
```

```python
import functools
import math

import jax
import jax.numpy as jnp
from jax import lax
from jax.experimental import pallas as pl
from jax.experimental.pallas import tpu as pltpu
from jax.sharding import PartitionSpec as P

CONV_DILATION = 3
PLANE = 4
LANES = 128
HALO = 16
EPS = 1e-06


def kernel(n, n_segment, hidden, owner, slot, table, key_weight, value_weight, taps, out,
           tab, hot, codes, stage, landed, own, packed, hid, kw, vw, tp, keys, values, normed, edge_out, edge_in, res,
           code_s, code_r, own_s, own_r, fwd_s, fwd_r, z_s, z_r, halo_s, halo_r, out_s, out_r, tab_l, in_l):
    me = lax.axis_index("table")
    seg = lax.axis_index("segment")
    groups = n // PLANE
    rows = table.shape[0]
    chunks = table.shape[1] // LANES
    tokens, features = hid.shape
    blocks = out_s.shape[0]
    block = tokens // blocks
    kernel_taps = taps.shape[0]

    near = me + 1 - 2 * (me % 2)
    side = me + 2 - 4 * ((me // 2) % 2)
    diag = side + 1 - 2 * (side % 2)
    after, before = (me + 1) % n, (me + n - 1) % n
    seg_after, seg_before = (seg + 1) % n_segment, (seg + n_segment - 1) % n_segment

    def peer(k):
        return (me + PLANE * k) % n

    def remote(src, dst, send, recv, **where):
        return pltpu.make_async_remote_copy(src_ref=src, dst_ref=dst, send_sem=send, recv_sem=recv,
                                            device_id=where, device_id_type=pl.DeviceIdType.MESH)

    barrier = pltpu.get_barrier_semaphore()
    for other in [near, side, after, before] + [peer(k) for k in range(1, groups)]:
        pl.semaphore_signal(barrier, inc=1, device_id={"table": other}, device_id_type=pl.DeviceIdType.MESH)
    for other in (seg_after, seg_before):
        pl.semaphore_signal(barrier, inc=1, device_id={"segment": other}, device_id_type=pl.DeviceIdType.MESH)

    def fetch(c):
        return pltpu.make_async_copy(table.at[:, pl.ds(c * LANES, LANES)], tab.at[c, pl.ds(0, rows)], tab_l.at[c])

    for c in range(chunks):
        fetch(c).start()
    inputs = [pltpu.make_async_copy(src, dst, in_l.at[i]) for i, (src, dst) in enumerate(
        [(hidden, hid), (key_weight, kw), (value_weight, vw), (taps, tp)])]
    for copy in inputs:
        copy.start()
    codes[0] = owner[...] * rows + slot[...]

    pl.semaphore_wait(barrier, 4 + groups - 1 + 2)

    def code_copy(k):
        return remote(codes.at[0], codes.at[groups - k], code_s.at[k], code_r.at[groups - k], table=peer(k))

    def own_copy(c, q):
        return remote(tab.at[c, pl.ds(0, rows)], tab.at[c, pl.ds(q * rows, rows)],
                      own_s.at[c, q], own_r.at[c, q], table=near if q == 1 else side)

    half = rows // 2

    def fwd_copy(c, q):
        at = 0 if q == 1 else half
        return remote(tab.at[c, pl.ds(q * rows + at, half)], tab.at[c, pl.ds(3 * rows + at, half)],
                      fwd_s.at[c, q], fwd_r.at[c, q], table=side if q == 1 else near)

    def z_copy(c, k):
        return remote(stage.at[c, k], landed.at[c, k], z_s.at[c, k], z_r.at[c, k], table=peer(k))

    def send_own(c):
        if c < chunks:
            fetch(c).wait()
            for q in (1, 2):
                own_copy(c, q).start()

    def forward(c):
        if c < chunks:
            for q in (1, 2):
                own_copy(c, q).wait_recv()
                fwd_copy(c, q).start()

    for k in range(1, groups):
        code_copy(k).start()
    send_own(0)
    send_own(1)

    lane = lax.broadcasted_iota(jnp.int32, (tokens, rows), 1)

    def mark(k):
        found = []
        for shard in (me, near, side, diag):
            offset = codes[k] - shard * rows
            inside = (offset >= 0) & (offset < rows)
            found.append(jnp.sum(jnp.where(inside, offset + 1, 0), axis=0, keepdims=True) - 1)
        column = jnp.concatenate(found + found, axis=0).astype(jnp.float32).T.astype(jnp.int32)
        for q in range(PLANE):
            hot[k, :, q * rows:(q + 1) * rows] = jnp.where(lane == column[:, q:q + 1], 1.0, 0.0).astype(jnp.bfloat16)

    mark(0)
    for k in range(1, groups):
        code_copy(k).wait_recv()

    @pl.loop(1, groups)
    def _(k):
        mark(k)

    forward(0)
    send_own(2)
    for c in range(chunks):
        forward(c + 1)
        send_own(c + 3)
        for q in (1, 2):
            fwd_copy(c, q).wait_recv()

        @pl.loop(1, groups)
        def _(k):
            stage[c, k] = jnp.dot(hot[k], tab[c], preferred_element_type=jnp.float32).astype(jnp.bfloat16)
            z_copy(c, k).start()

        own[c] = jnp.dot(hot[0], tab[c], preferred_element_type=jnp.float32)

    for copy in inputs:
        copy.wait()
    for c in range(chunks):
        for k in range(1, groups):
            z_copy(c, k).wait_recv()
        total = own[c]
        for k in range(1, groups):
            total = total + landed[c, k].astype(jnp.float32)
        packed[:, c * LANES:(c + 1) * LANES] = total.astype(jnp.bfloat16)

    keys[...] = jnp.dot(packed[...], kw[...], preferred_element_type=jnp.float32)
    values[...] = jnp.dot(packed[...], vw[...], preferred_element_type=jnp.float32)

    halo = remote(edge_out, edge_in, halo_s, halo_r, table=after)

    def gates(b):
        here = pl.ds(b * block, block)
        states = hid[here, :].astype(jnp.float32)
        key = keys[here, :]
        value = values[here, :]

        def mean(x):
            return jnp.sum(x, axis=-1, keepdims=True) / features

        affinity = (jnp.sum(states * key, axis=-1, keepdims=True)
                    * lax.rsqrt(mean(states * states) + EPS) * lax.rsqrt(mean(key * key) + EPS)) / math.sqrt(features)
        gated = value * jax.nn.sigmoid(affinity)
        scaled = gated * lax.rsqrt(mean(gated * gated) + EPS)
        normed[pl.ds(HALO + b * block, block), :] = scaled
        values[here, :] = gated
        if b == blocks - 1:
            edge_out[...] = scaled[block - HALO:].astype(jnp.bfloat16)
            halo.start()

    def out_copy(b):
        here = pl.ds(b * block, block)
        return remote(res.at[here, :], out.at[here, :], out_s.at[b], out_r.at[b], segment=seg_after)

    def finish(b):
        here = pl.ds(b * block, block)
        mixed = tp[0:1, :] * normed[pl.ds(HALO + b * block, block), :]
        for tap in range(1, kernel_taps):
            mixed = mixed + tp[tap:tap + 1, :] * normed[pl.ds(HALO + b * block - tap * CONV_DILATION, block), :]
        total = hid[here, :].astype(jnp.float32) + (mixed * jax.nn.sigmoid(mixed) + values[here, :])
        res[here, :] = total.astype(jnp.bfloat16)
        out_copy(b).start()

    gates(blocks - 1)
    for b in range(blocks - 1):
        gates(b)
    for b in range(1, blocks):
        finish(b)
    halo.wait_recv()
    normed[pl.ds(0, HALO), :] = jnp.where(me > 0, edge_in[...].astype(jnp.float32), 0.0)
    finish(0)

    for k in range(1, groups):
        code_copy(k).wait_send()
    for c in range(chunks):
        for q in (1, 2):
            own_copy(c, q).wait_send()
            fwd_copy(c, q).wait_send()
        for k in range(1, groups):
            z_copy(c, k).wait_send()
    halo.wait_send()
    for b in range(blocks):
        out_copy(b).wait()


def local(n, n_segment, hidden, owner, slot, memory_table, key_weight, value_weight, conv_weight):
    tokens, features = hidden.shape[1:]
    heads = owner.shape[2]
    rows, width = memory_table.shape[1:]
    kernel_taps = conv_weight.shape[1]
    groups, chunks, blocks = n // PLANE, width // LANES, 8
    bf, f32 = jnp.bfloat16, jnp.float32
    dma = pltpu.SemaphoreType.DMA
    anywhere, vmem = pl.BlockSpec(memory_space=pl.ANY), pl.BlockSpec(memory_space=pltpu.VMEM)
    result = pl.pallas_call(
        functools.partial(kernel, n, n_segment),
        out_shape=jax.ShapeDtypeStruct((tokens, features), bf),
        in_specs=[anywhere, vmem, vmem, anywhere, anywhere, anywhere, anywhere],
        out_specs=anywhere,
        scratch_shapes=[
            pltpu.VMEM((chunks, PLANE * rows, LANES), bf),
            pltpu.VMEM((groups, tokens, PLANE * rows), bf),
            pltpu.VMEM((groups, heads, tokens), jnp.int32),
            pltpu.VMEM((chunks, groups, tokens, LANES), bf),
            pltpu.VMEM((chunks, groups, tokens, LANES), bf),
            pltpu.VMEM((chunks, tokens, LANES), f32),
            pltpu.VMEM((tokens, width), bf),
            pltpu.VMEM((tokens, features), bf),
            pltpu.VMEM((width, features), bf),
            pltpu.VMEM((width, features), bf),
            pltpu.VMEM((kernel_taps, features), f32),
            pltpu.VMEM((tokens, features), f32),
            pltpu.VMEM((tokens, features), f32),
            pltpu.VMEM((HALO + tokens, features), f32),
            pltpu.VMEM((HALO, features), bf),
            pltpu.VMEM((HALO, features), bf),
            pltpu.VMEM((tokens, features), bf),
            dma((groups,)), dma((groups,)),
            dma((chunks, 3)), dma((chunks, 3)),
            dma((chunks, 3)), dma((chunks, 3)),
            dma((chunks, groups)), dma((chunks, groups)),
            dma, dma,
            dma((blocks,)), dma((blocks,)),
            dma((chunks,)), dma((4,)),
        ],
        compiler_params=pltpu.CompilerParams(collective_id=0, has_side_effects=True, vmem_limit_bytes=48 << 20),
    )(hidden[0], owner[0].T, slot[0].T, memory_table[0], key_weight[0], value_weight[0], conv_weight[0])
    return result[None]


def solution(mesh):
    in_specs = (
        P("segment", "table", None),
        P("segment", "table", None),
        P("segment", "table", None),
        P("segment", "table", None),
        P("segment", None, None),
        P("segment", None, None),
        P("segment", None, None),
    )
    out_specs = P("segment", "table", None)
    step = functools.partial(local, mesh.shape["table"], mesh.shape["segment"])
    return jax.shard_map(step, mesh=mesh, in_specs=in_specs, out_specs=out_specs, check_vma=False)
```

```python
import functools
import math

import jax
import jax.numpy as jnp
from jax import lax
from jax.experimental import pallas as pl
from jax.experimental.pallas import tpu as pltpu
from jax.sharding import PartitionSpec as P

CONV_DILATION = 3
PLANE = 4
LANES = 128
HALO = 16
EPS = 1e-06


def kernel(n, n_segment, hidden, owner, slot, table, key_weight, value_weight, taps, out,
           tab, hot, codes, stage, landed, own, packed, hid, kw, vw, tp, keys, values, normed, edge_out, edge_in, res, relay, own_code, own_slot,
           code_s, code_r, own_s, own_r, fwd_s, fwd_r, z_s, z_r, halo_s, halo_r, out_s, out_r, tab_l, in_l, relay_s, relay_r):
    me = lax.axis_index("table")
    seg = lax.axis_index("segment")
    groups = n // PLANE
    rows = table.shape[0]
    chunks = table.shape[1] // LANES
    tokens, features = hid.shape
    blocks = out_s.shape[0]
    block = tokens // blocks
    kernel_taps = taps.shape[0]

    near = me + 1 - 2 * (me % 2)
    side = me + 2 - 4 * ((me // 2) % 2)
    diag = side + 1 - 2 * (side % 2)
    after, before = (me + 1) % n, (me + n - 1) % n
    seg_after, seg_before = (seg + 1) % n_segment, (seg + n_segment - 1) % n_segment

    group = me // PLANE
    line = groups == 4
    end = group % 3 == 0

    def peer(k):
        if not line:
            return (me + PLANE * k) % n
        other = {1: group + 1 - 2 * (group % 2), 2: group + 2 - 4 * (group // 2), 3: 3 - group}[k]
        return other * PLANE + me % PLANE

    def remote(src, dst, send, recv, **where):
        return pltpu.make_async_remote_copy(src_ref=src, dst_ref=dst, send_sem=send, recv_sem=recv,
                                            device_id=where, device_id_type=pl.DeviceIdType.MESH)

    barrier = pltpu.get_barrier_semaphore()
    for other in [near, side, after, before] + [peer(k) for k in range(1, groups)]:
        pl.semaphore_signal(barrier, inc=1, device_id={"table": other}, device_id_type=pl.DeviceIdType.MESH)
    for other in (seg_after, seg_before):
        pl.semaphore_signal(barrier, inc=1, device_id={"segment": other}, device_id_type=pl.DeviceIdType.MESH)

    def fetch(c):
        return pltpu.make_async_copy(table.at[:, pl.ds(c * LANES, LANES)], tab.at[c, pl.ds(0, rows)], tab_l.at[c])

    inputs = [pltpu.make_async_copy(src, dst, in_l.at[i]) for i, (src, dst) in enumerate(
        [(owner, own_code), (slot, own_slot), (hidden, hid), (key_weight, kw), (value_weight, vw), (taps, tp)])]
    for copy in inputs[:2]:
        copy.start()
    for c in range(chunks):
        fetch(c).start()
    for copy in inputs[2:]:
        copy.start()
    for copy in inputs[:2]:
        copy.wait()
    codes[0] = own_code[...] * rows + own_slot[...]

    pl.semaphore_wait(barrier, 4 + groups - 1 + 2)

    def code_copy(k):
        there = k if line else groups - k
        return remote(codes.at[0], codes.at[there], code_s.at[k], code_r.at[there], table=peer(k))

    def own_copy(c, q):
        return remote(tab.at[c, pl.ds(0, rows)], tab.at[c, pl.ds(q * rows, rows)],
                      own_s.at[c, q], own_r.at[c, q], table=near if q == 1 else side)

    half = rows // 2

    def fwd_copy(c, q):
        at = 0 if q == 1 else half
        return remote(tab.at[c, pl.ds(q * rows + at, half)], tab.at[c, pl.ds(3 * rows + at, half)],
                      fwd_s.at[c, q], fwd_r.at[c, q], table=side if q == 1 else near)

    def z_copy(c, k):
        return remote(stage.at[c, k], landed.at[c, k], z_s.at[c, k], z_r.at[c, k], table=peer(k))

    def relay_copy(c):
        return remote(stage.at[c, 3], relay.at[c], relay_s.at[c], relay_r.at[c], table=peer(1))

    def look(c, k):
        return jnp.dot(hot[k], tab[c], preferred_element_type=jnp.float32)

    def send_sums(c, k):
        stage[c, k] = look(c, k).astype(jnp.bfloat16)
        z_copy(c, k).start()

    def send_far(c):
        if line:
            @pl.when(jnp.logical_not(end))
            def _():
                relay_copy(c).wait_recv()
                stage[c, 2] = (look(c, 2) + relay[c].astype(jnp.float32)).astype(jnp.bfloat16)
                z_copy(c, 2).start()

    def send_own(c):
        if c < chunks:
            fetch(c).wait()
            for q in (1, 2):
                own_copy(c, q).start()

    def forward(c):
        if c < chunks:
            for q in (1, 2):
                own_copy(c, q).wait_recv()
                fwd_copy(c, q).start()

    for k in range(1, groups):
        code_copy(k).start()
    send_own(0)
    send_own(1)

    lane = lax.broadcasted_iota(jnp.int32, (tokens, rows), 1)

    def mark(k):
        found = []
        for shard in (me, near, side, diag):
            offset = codes[k] - shard * rows
            inside = (offset >= 0) & (offset < rows)
            found.append(jnp.sum(jnp.where(inside, offset + 1, 0), axis=0, keepdims=True) - 1)
        column = jnp.concatenate(found + found, axis=0).astype(jnp.float32).T.astype(jnp.int32)
        for q in range(PLANE):
            hot[k, :, q * rows:(q + 1) * rows] = jnp.where(lane == column[:, q:q + 1], 1.0, 0.0).astype(jnp.bfloat16)

    mark(0)
    for k in range(1, groups):
        code_copy(k).wait_recv()

    @pl.loop(1, groups)
    def _(k):
        mark(k)

    forward(0)
    send_own(2)
    for c in range(chunks):
        forward(c + 1)
        send_own(c + 3)
        for q in (1, 2):
            fwd_copy(c, q).wait_recv()

        if line:
            @pl.when(end)
            def _():
                stage[c, 3] = look(c, 3).astype(jnp.bfloat16)
                relay_copy(c).start()
                send_sums(c, 2)

            @pl.when(jnp.logical_not(end))
            def _():
                send_sums(c, 3)

            if c > 0:
                send_far(c - 1)
            send_sums(c, 1)
        else:
            @pl.loop(1, groups)
            def _(k):
                send_sums(c, k)

        own[c] = look(c, 0)
    send_far(chunks - 1)

    for copy in inputs[2:]:
        copy.wait()

    def collect(c):
        def add(ks):
            for k in ks:
                z_copy(c, k).wait_recv()
            total = own[c]
            for k in ks:
                total = total + landed[c, k].astype(jnp.float32)
            packed[:, c * LANES:(c + 1) * LANES] = total.astype(jnp.bfloat16)

        if line:
            @pl.when(end)
            def _():
                add((1, 2))

            @pl.when(jnp.logical_not(end))
            def _():
                add((1, 3, 2))
        else:
            add(range(1, groups))

    for c in range(chunks - 1):
        collect(c)
    early = (chunks - 1) * LANES
    for weight, product in ((kw, keys), (vw, values)):
        product[...] = jnp.dot(packed[:, :early], weight[:early, :], preferred_element_type=jnp.float32)
    collect(chunks - 1)
    for weight, product in ((kw, keys), (vw, values)):
        product[...] += jnp.dot(packed[:, early:], weight[early:, :], preferred_element_type=jnp.float32)

    halo = remote(edge_out, edge_in, halo_s, halo_r, table=after)

    def gates(b):
        here = pl.ds(b * block, block)
        states = hid[here, :].astype(jnp.float32)
        key = keys[here, :]
        value = values[here, :]

        def mean(x):
            return jnp.sum(x, axis=-1, keepdims=True) / features

        affinity = (jnp.sum(states * key, axis=-1, keepdims=True)
                    * lax.rsqrt(mean(states * states) + EPS) * lax.rsqrt(mean(key * key) + EPS)) / math.sqrt(features)
        gated = value * jax.nn.sigmoid(affinity)
        scaled = gated * lax.rsqrt(mean(gated * gated) + EPS)
        normed[pl.ds(HALO + b * block, block), :] = scaled
        values[here, :] = gated
        if b == blocks - 1:
            edge_out[...] = scaled[block - HALO:].astype(jnp.bfloat16)
            halo.start()

    def out_copy(b):
        here = pl.ds(b * block, block)
        return remote(res.at[here, :], out.at[here, :], out_s.at[b], out_r.at[b], segment=seg_after)

    def finish(b):
        here = pl.ds(b * block, block)
        mixed = tp[0:1, :] * normed[pl.ds(HALO + b * block, block), :]
        for tap in range(1, kernel_taps):
            mixed = mixed + tp[tap:tap + 1, :] * normed[pl.ds(HALO + b * block - tap * CONV_DILATION, block), :]
        total = hid[here, :].astype(jnp.float32) + (mixed * jax.nn.sigmoid(mixed) + values[here, :])
        res[here, :] = total.astype(jnp.bfloat16)
        out_copy(b).start()

    gates(blocks - 1)
    for b in range(blocks - 1):
        gates(b)
    for b in range(1, blocks):
        finish(b)
    halo.wait_recv()
    normed[pl.ds(0, HALO), :] = jnp.where(me > 0, edge_in[...].astype(jnp.float32), 0.0)
    finish(0)

    for k in range(1, groups):
        code_copy(k).wait_send()
    for c in range(chunks):
        for q in (1, 2):
            own_copy(c, q).wait_send()
            fwd_copy(c, q).wait_send()
        for k in range(1, 3 if line else groups):
            z_copy(c, k).wait_send()
        if line:
            @pl.when(end)
            def _():
                relay_copy(c).wait_send()

            @pl.when(jnp.logical_not(end))
            def _():
                z_copy(c, 3).wait_send()
    halo.wait_send()
    for b in range(blocks):
        out_copy(b).wait()


def local(n, n_segment, hidden, owner, slot, memory_table, key_weight, value_weight, conv_weight):
    tokens, features = hidden.shape[1:]
    heads = owner.shape[2]
    rows, width = memory_table.shape[1:]
    kernel_taps = conv_weight.shape[1]
    groups, chunks, blocks = n // PLANE, width // LANES, 8
    bf, f32 = jnp.bfloat16, jnp.float32
    dma = pltpu.SemaphoreType.DMA
    anywhere = pl.BlockSpec(memory_space=pl.ANY)
    result = pl.pallas_call(
        functools.partial(kernel, n, n_segment),
        out_shape=jax.ShapeDtypeStruct((tokens, features), bf),
        in_specs=[anywhere] * 7,
        out_specs=anywhere,
        scratch_shapes=[
            pltpu.VMEM((chunks, PLANE * rows, LANES), bf),
            pltpu.VMEM((groups, tokens, PLANE * rows), bf),
            pltpu.VMEM((groups, heads, tokens), jnp.int32),
            pltpu.VMEM((chunks, groups, tokens, LANES), bf),
            pltpu.VMEM((chunks, groups, tokens, LANES), bf),
            pltpu.VMEM((chunks, tokens, LANES), f32),
            pltpu.VMEM((tokens, width), bf),
            pltpu.VMEM((tokens, features), bf),
            pltpu.VMEM((width, features), bf),
            pltpu.VMEM((width, features), bf),
            pltpu.VMEM((kernel_taps, features), f32),
            pltpu.VMEM((tokens, features), f32),
            pltpu.VMEM((tokens, features), f32),
            pltpu.VMEM((HALO + tokens, features), f32),
            pltpu.VMEM((HALO, features), bf),
            pltpu.VMEM((HALO, features), bf),
            pltpu.VMEM((tokens, features), bf),
            pltpu.VMEM((chunks, tokens, LANES), bf),
            pltpu.VMEM((heads, tokens), jnp.int32),
            pltpu.VMEM((heads, tokens), jnp.int32),
            dma((groups,)), dma((groups,)),
            dma((chunks, 3)), dma((chunks, 3)),
            dma((chunks, 3)), dma((chunks, 3)),
            dma((chunks, groups)), dma((chunks, groups)),
            dma, dma,
            dma((blocks,)), dma((blocks,)),
            dma((chunks,)), dma((6,)),
            dma((chunks,)), dma((chunks,)),
        ],
        compiler_params=pltpu.CompilerParams(collective_id=0, has_side_effects=True, vmem_limit_bytes=62 << 20),
    )(hidden[0], owner[0].T, slot[0].T, memory_table[0], key_weight[0], value_weight[0], conv_weight[0])
    return result[None]


def solution(mesh):
    in_specs = (
        P("segment", "table", None),
        P("segment", "table", None),
        P("segment", "table", None),
        P("segment", "table", None),
        P("segment", None, None),
        P("segment", None, None),
        P("segment", None, None),
    )
    out_specs = P("segment", "table", None)
    step = functools.partial(local, mesh.shape["table"], mesh.shape["segment"])
    return jax.shard_map(step, mesh=mesh, in_specs=in_specs, out_specs=out_specs, check_vma=False)
```

```python
import functools
import math

import jax
import jax.numpy as jnp
from jax import lax
from jax.experimental import pallas as pl
from jax.experimental.pallas import tpu as pltpu
from jax.sharding import PartitionSpec as P

CONV_DILATION = 3
PLANE = 4
LANES = 128
HALO = 16
EPS = 1e-06


def kernel(n, n_segment, hidden, owner, slot, table, key_weight, value_weight, taps, out,
           tab, hot, codes, stage, landed, own, packed, hid, kw, vw, tp, keys, values, normed, edge_out, edge_in, res, relay, own_code, own_slot,
           code_s, code_r, own_s, own_r, fwd_s, fwd_r, z_s, z_r, halo_s, halo_r, out_s, out_r, tab_l, in_l, relay_s, relay_r):
    me = lax.axis_index("table")
    seg = lax.axis_index("segment")
    groups = n // PLANE
    rows = table.shape[0]
    chunks = table.shape[1] // LANES
    tokens, features = hid.shape
    blocks = out_s.shape[0]
    block = tokens // blocks
    kernel_taps = taps.shape[0]

    near = me + 1 - 2 * (me % 2)
    side = me + 2 - 4 * ((me // 2) % 2)
    diag = side + 1 - 2 * (side % 2)
    after, before = (me + 1) % n, (me + n - 1) % n
    seg_after, seg_before = (seg + 1) % n_segment, (seg + n_segment - 1) % n_segment

    group = me // PLANE
    line = groups == 4
    end = group % 3 == 0

    def peer(k):
        if not line:
            return (me + PLANE * k) % n
        other = {1: group + 1 - 2 * (group % 2), 2: group + 2 - 4 * (group // 2), 3: 3 - group}[k]
        return other * PLANE + me % PLANE

    def remote(src, dst, send, recv, **where):
        return pltpu.make_async_remote_copy(src_ref=src, dst_ref=dst, send_sem=send, recv_sem=recv,
                                            device_id=where, device_id_type=pl.DeviceIdType.MESH)

    barrier = pltpu.get_barrier_semaphore()
    for other in [near, side, after, before] + [peer(k) for k in range(1, groups)]:
        pl.semaphore_signal(barrier, inc=1, device_id={"table": other}, device_id_type=pl.DeviceIdType.MESH)
    for other in (seg_after, seg_before):
        pl.semaphore_signal(barrier, inc=1, device_id={"segment": other}, device_id_type=pl.DeviceIdType.MESH)

    def fetch(c):
        return pltpu.make_async_copy(table.at[:, pl.ds(c * LANES, LANES)], tab.at[c, pl.ds(0, rows)], tab_l.at[c])

    inputs = [pltpu.make_async_copy(src, dst, in_l.at[i]) for i, (src, dst) in enumerate(
        [(owner, own_code), (slot, own_slot), (hidden, hid), (key_weight, kw), (value_weight, vw), (taps, tp)])]
    for copy in inputs[:2]:
        copy.start()
    for c in range(chunks):
        fetch(c).start()
    for copy in inputs[2:]:
        copy.start()
    for copy in inputs[:2]:
        copy.wait()
    codes[0] = own_code[...] * rows + own_slot[...]

    pl.semaphore_wait(barrier, 4 + groups - 1 + 2)

    def code_copy(k):
        there = k if line else groups - k
        return remote(codes.at[0], codes.at[there], code_s.at[k], code_r.at[there], table=peer(k))

    def own_copy(c, q):
        return remote(tab.at[c, pl.ds(0, rows)], tab.at[c, pl.ds(q * rows, rows)],
                      own_s.at[c, q], own_r.at[c, q], table=near if q == 1 else side)

    half = rows // 2

    def fwd_copy(c, q):
        at = 0 if q == 1 else half
        return remote(tab.at[c, pl.ds(q * rows + at, half)], tab.at[c, pl.ds(3 * rows + at, half)],
                      fwd_s.at[c, q], fwd_r.at[c, q], table=side if q == 1 else near)

    def z_copy(c, k):
        return remote(stage.at[c, k], landed.at[c, k], z_s.at[c, k], z_r.at[c, k], table=peer(k))

    def relay_copy(c):
        return remote(stage.at[c, 3], relay.at[c], relay_s.at[c], relay_r.at[c], table=peer(1))

    def look(c, k):
        return jnp.dot(hot[k], tab[c], preferred_element_type=jnp.float32)

    def send_sums(c, k):
        stage[c, k] = look(c, k).astype(jnp.bfloat16)
        z_copy(c, k).start()

    def send_far(c):
        if line:
            @pl.when(jnp.logical_not(end))
            def _():
                relay_copy(c).wait_recv()
                stage[c, 2] = (look(c, 2) + relay[c].astype(jnp.float32)).astype(jnp.bfloat16)
                z_copy(c, 2).start()

    def send_own(c):
        if c < chunks:
            fetch(c).wait()
            for q in (1, 2):
                own_copy(c, q).start()

    def forward(c):
        if c < chunks:
            for q in (1, 2):
                own_copy(c, q).wait_recv()
                fwd_copy(c, q).start()

    for k in range(1, groups):
        code_copy(k).start()
    send_own(0)
    send_own(1)

    lane = lax.broadcasted_iota(jnp.int32, (tokens, rows), 1)

    def mark(k):
        found = []
        for shard in (me, near, side, diag):
            offset = codes[k] - shard * rows
            inside = (offset >= 0) & (offset < rows)
            found.append(jnp.sum(jnp.where(inside, offset + 1, 0), axis=0, keepdims=True) - 1)
        column = jnp.concatenate(found + found, axis=0).astype(jnp.float32).T.astype(jnp.int32)
        for q in range(PLANE):
            hot[k, :, q * rows:(q + 1) * rows] = jnp.where(lane == column[:, q:q + 1], 1.0, 0.0).astype(jnp.bfloat16)

    mark(0)
    forward(0)
    send_own(2)
    for k in range(1, groups):
        code_copy(k).wait_recv()

    @pl.loop(1, groups)
    def _(k):
        mark(k)

    for c in range(chunks):
        forward(c + 1)
        send_own(c + 3)
        for q in (1, 2):
            fwd_copy(c, q).wait_recv()

        if line:
            @pl.when(end)
            def _():
                stage[c, 3] = look(c, 3).astype(jnp.bfloat16)
                relay_copy(c).start()
                send_sums(c, 2)

            @pl.when(jnp.logical_not(end))
            def _():
                send_sums(c, 3)

            if c > 0:
                send_far(c - 1)
            send_sums(c, 1)
        else:
            @pl.loop(1, groups)
            def _(k):
                send_sums(c, k)

        own[c] = look(c, 0)
    send_far(chunks - 1)

    for copy in inputs[2:]:
        copy.wait()

    def collect(c):
        def add(ks):
            for k in ks:
                z_copy(c, k).wait_recv()
            total = own[c]
            for k in ks:
                total = total + landed[c, k].astype(jnp.float32)
            packed[:, c * LANES:(c + 1) * LANES] = total.astype(jnp.bfloat16)

        if line:
            @pl.when(end)
            def _():
                add((1, 2))

            @pl.when(jnp.logical_not(end))
            def _():
                add((1, 3, 2))
        else:
            add(range(1, groups))

    for c in range(chunks - 1):
        collect(c)
    early = (chunks - 1) * LANES
    for weight, product in ((kw, keys), (vw, values)):
        product[...] = jnp.dot(packed[:, :early], weight[:early, :], preferred_element_type=jnp.float32)
    collect(chunks - 1)
    for weight, product in ((kw, keys), (vw, values)):
        product[...] += jnp.dot(packed[:, early:], weight[early:, :], preferred_element_type=jnp.float32)

    halo = remote(edge_out, edge_in, halo_s, halo_r, table=after)

    def gates(b):
        here = pl.ds(b * block, block)
        states = hid[here, :].astype(jnp.float32)
        key = keys[here, :]
        value = values[here, :]

        def mean(x):
            return jnp.sum(x, axis=-1, keepdims=True) / features

        affinity = (jnp.sum(states * key, axis=-1, keepdims=True)
                    * lax.rsqrt(mean(states * states) + EPS) * lax.rsqrt(mean(key * key) + EPS)) / math.sqrt(features)
        gated = value * jax.nn.sigmoid(affinity)
        scaled = gated * lax.rsqrt(mean(gated * gated) + EPS)
        normed[pl.ds(HALO + b * block, block), :] = scaled
        values[here, :] = gated
        if b == blocks - 1:
            edge_out[...] = scaled[block - HALO:].astype(jnp.bfloat16)

            @pl.when(me < n - 1)
            def _():
                halo.start()

    def out_copy(b):
        here = pl.ds(b * block, block)
        return remote(res.at[here, :], out.at[here, :], out_s.at[b], out_r.at[b], segment=seg_after)

    def finish(b):
        here = pl.ds(b * block, block)
        mixed = tp[0:1, :] * normed[pl.ds(HALO + b * block, block), :]
        for tap in range(1, kernel_taps):
            mixed = mixed + tp[tap:tap + 1, :] * normed[pl.ds(HALO + b * block - tap * CONV_DILATION, block), :]
        total = hid[here, :].astype(jnp.float32) + (mixed * jax.nn.sigmoid(mixed) + values[here, :])
        res[here, :] = total.astype(jnp.bfloat16)
        out_copy(b).start()

    gates(blocks - 1)
    for b in range(blocks - 1):
        gates(b)
    for b in range(1, blocks):
        finish(b)

    @pl.when(me > 0)
    def _():
        halo.wait_recv()
        normed[pl.ds(0, HALO), :] = edge_in[...].astype(jnp.float32)

    @pl.when(me == 0)
    def _():
        normed[pl.ds(0, HALO), :] = jnp.zeros((HALO, features), jnp.float32)

    finish(0)

    for k in range(1, groups):
        code_copy(k).wait_send()
    for c in range(chunks):
        for q in (1, 2):
            own_copy(c, q).wait_send()
            fwd_copy(c, q).wait_send()
        for k in range(1, 3 if line else groups):
            z_copy(c, k).wait_send()
        if line:
            @pl.when(end)
            def _():
                relay_copy(c).wait_send()

            @pl.when(jnp.logical_not(end))
            def _():
                z_copy(c, 3).wait_send()

    @pl.when(me < n - 1)
    def _():
        halo.wait_send()

    for b in range(blocks):
        out_copy(b).wait()


def local(n, n_segment, hidden, owner, slot, memory_table, key_weight, value_weight, conv_weight):
    tokens, features = hidden.shape[1:]
    heads = owner.shape[2]
    rows, width = memory_table.shape[1:]
    kernel_taps = conv_weight.shape[1]
    groups, chunks, blocks = n // PLANE, width // LANES, 8
    bf, f32 = jnp.bfloat16, jnp.float32
    dma = pltpu.SemaphoreType.DMA
    anywhere = pl.BlockSpec(memory_space=pl.ANY)
    result = pl.pallas_call(
        functools.partial(kernel, n, n_segment),
        out_shape=jax.ShapeDtypeStruct((tokens, features), bf),
        in_specs=[anywhere] * 7,
        out_specs=anywhere,
        scratch_shapes=[
            pltpu.VMEM((chunks, PLANE * rows, LANES), bf),
            pltpu.VMEM((groups, tokens, PLANE * rows), bf),
            pltpu.VMEM((groups, heads, tokens), jnp.int32),
            pltpu.VMEM((chunks, groups, tokens, LANES), bf),
            pltpu.VMEM((chunks, groups, tokens, LANES), bf),
            pltpu.VMEM((chunks, tokens, LANES), f32),
            pltpu.VMEM((tokens, width), bf),
            pltpu.VMEM((tokens, features), bf),
            pltpu.VMEM((width, features), bf),
            pltpu.VMEM((width, features), bf),
            pltpu.VMEM((kernel_taps, features), f32),
            pltpu.VMEM((tokens, features), f32),
            pltpu.VMEM((tokens, features), f32),
            pltpu.VMEM((HALO + tokens, features), f32),
            pltpu.VMEM((HALO, features), bf),
            pltpu.VMEM((HALO, features), bf),
            pltpu.VMEM((tokens, features), bf),
            pltpu.VMEM((chunks, tokens, LANES), bf),
            pltpu.VMEM((heads, tokens), jnp.int32),
            pltpu.VMEM((heads, tokens), jnp.int32),
            dma((groups,)), dma((groups,)),
            dma((chunks, 3)), dma((chunks, 3)),
            dma((chunks, 3)), dma((chunks, 3)),
            dma((chunks, groups)), dma((chunks, groups)),
            dma, dma,
            dma((blocks,)), dma((blocks,)),
            dma((chunks,)), dma((6,)),
            dma((chunks,)), dma((chunks,)),
        ],
        compiler_params=pltpu.CompilerParams(collective_id=0, has_side_effects=True, vmem_limit_bytes=62 << 20),
    )(hidden[0], owner[0].T, slot[0].T, memory_table[0], key_weight[0], value_weight[0], conv_weight[0])
    return result[None]


def solution(mesh):
    in_specs = (
        P("segment", "table", None),
        P("segment", "table", None),
        P("segment", "table", None),
        P("segment", "table", None),
        P("segment", None, None),
        P("segment", None, None),
        P("segment", None, None),
    )
    out_specs = P("segment", "table", None)
    step = functools.partial(local, mesh.shape["table"], mesh.shape["segment"])
    return jax.shard_map(step, mesh=mesh, in_specs=in_specs, out_specs=out_specs, check_vma=False)
```
